32 devices in a mesh: gx: 4 (over y, core), gy: 8 (over z, x).
Axes of the slice: x: 2, y: 2, z: 4, core: 2. Of those that a mesh axis runs over, the one named last changes fastest.
Arguments:
- entity_table: float32 [8192, 256], P(('gx', 'gy')), may hold values from -2.5 to 2.5
- relations: float32 [4, 256, 256], replicated, may hold values from -0.375 to 0.375
- rel_ids: int32 [3, 128], P(None, ('gx', 'gy')), may hold values from 0 to 3
- edge_src: int32 [3, 196608], P(None, ('gx', 'gy')), may hold values from 0 to 255
- edge_dst: int32 [3, 196608], P(None, ('gx', 'gy')), may hold values from 0 to 255
Outputs:
- new_table: float32 [8192, 256], P(('gx', 'gy'))
- rel_grad: float32 [4, 256, 256], replicated
The draws below stay inside these ranges and needn't reach their ends.
All inputs are finite; a program needn't handle non-finite values.
Results may differ from the reference program's by a relative error of at most 0.0089.
Values may be sent and summed in bfloat16 or wider, within the bound.
A program may use at most 64 MiB of HBM per device.

```python
import math
import jax
import jax.numpy as jnp
from jax import lax

D = 256
REL = 4
GROUPS = 4
ROUNDS = 3
ROWS = 256
EDGES_DEV = 6144
ENTITIES = 8192
GROUP_ALL = 128
EDGE_ALL = 196608
N_GX = 4
N_GY = 8


def with_ends(values, rng, least, high):
    spot = [jax.random.randint(jax.random.fold_in(rng, axis), (), 0, length) for axis, length in enumerate(values.shape)]
    main_axis = values.shape.index(max(values.shape))
    neighbour = spot[:main_axis] + [(spot[main_axis] + 1) % values.shape[main_axis]] + spot[main_axis + 1:]
    return values.at[tuple(spot)].set(least).at[tuple(neighbour)].set(high)


def level_of(rng, extent, shards, smallest, top_value):
    def one(dim, shards_of):
        draws = jax.random.uniform(jax.random.fold_in(jax.random.fold_in(rng, 6), dim), (shards_of,), jnp.float32, smallest / len(shards), top_value / len(shards))
        return jnp.repeat(jnp.exp(draws), extent[dim] // shards_of).reshape((-1,) + (1,) * (len(extent) - dim - 1))

    gain = one(*shards[0])
    for cut in shards[1:]:
        gain = gain * one(*cut)
    return gain


def scatter_about(rng, dims, deviation, limit, shards=(), kind=jnp.bfloat16):
    level = level_of(rng, dims, shards, -0.22, 0.18) if shards else 1.0
    drawn = jax.random.normal(rng, dims, jnp.float32) * deviation * level
    return jnp.minimum(jnp.maximum(drawn, -limit), limit).astype(kind)


def setup_inputs(seed: int = 0) -> dict:
    arg_keys = jax.random.split(jax.random.key(seed), 6)
    entity_table = scatter_about(arg_keys[0], (ENTITIES, D), 0.35, 2.5, ((0, 32),), jnp.float32)
    relations = scatter_about(arg_keys[1], (REL, D, D), D ** -0.5, 0.375, (), jnp.float32)
    rel_ids = with_ends(jax.random.randint(arg_keys[2], (ROUNDS, GROUP_ALL), 0, REL), jax.random.fold_in(arg_keys[2], 1), 0, REL - 1).astype(jnp.int32)
    edge_src = with_ends(jax.random.randint(arg_keys[3], (ROUNDS, EDGE_ALL), 0, ROWS), jax.random.fold_in(arg_keys[3], 1), 0, ROWS - 1).astype(jnp.int32)
    edge_dst = with_ends(jax.random.randint(arg_keys[4], (ROUNDS, EDGE_ALL), 0, ROWS), jax.random.fold_in(arg_keys[4], 1), 0, ROWS - 1).astype(jnp.int32)
    return {"entity_table": entity_table, "relations": relations, "rel_ids": rel_ids, "edge_src": edge_src, "edge_dst": edge_dst}


learn_rate = 0.5
highest = lax.Precision.HIGHEST

def bucket_terms(src_rows, dst_rows, relations, group_ids, sources, targets):
    row_count, feature = src_rows.shape
    group_count = group_ids.shape[0]
    kinds = relations.shape[0]
    selector = (group_ids[:, None] == jnp.arange(kinds, dtype=jnp.int32)[None, :]).astype(jnp.float32)
    chosen = jnp.einsum('gk,kde->gde', selector, relations, precision=highest).astype(jnp.bfloat16)
    src_b = src_rows.astype(jnp.bfloat16).reshape(group_count, row_count // group_count, feature)
    dst_b = dst_rows.astype(jnp.bfloat16)
    mapped = jnp.einsum('gsd,gde->gse', src_b.astype(jnp.float32), chosen.astype(jnp.float32), precision=highest).astype(jnp.bfloat16)
    mapped_flat = mapped.reshape(row_count, feature)
    scores = jnp.dot(mapped_flat, dst_b.T, preferred_element_type=jnp.float32)
    scaling = 1.0 / math.sqrt(row_count)
    slopes = jax.nn.sigmoid(scores) * scaling
    slopes = slopes.at[sources, targets].add(-scaling)
    slopes_b = slopes.astype(jnp.bfloat16)
    pulled = jnp.dot(slopes_b, dst_b, preferred_element_type=jnp.float32).astype(jnp.bfloat16)
    pulled = pulled.reshape(group_count, row_count // group_count, feature)
    src_grad = jnp.einsum('gse,gde->gsd', pulled.astype(jnp.float32), chosen.astype(jnp.float32), precision=highest).reshape(row_count, feature)
    dst_grad = jnp.dot(slopes_b.T, mapped_flat, preferred_element_type=jnp.float32).astype(jnp.bfloat16)
    dst_grad = lax.optimization_barrier(dst_grad).astype(jnp.float32)
    rel_group = jnp.einsum('gsd,gse->gde', src_b.astype(jnp.float32), pulled.astype(jnp.float32), precision=highest)
    rel_part = jnp.einsum('gk,gde->kde', selector, rel_group, precision=highest)
    return (src_grad, dst_grad, rel_part)

def reference(entity_table, relations, rel_ids, edge_src, edge_dst):
    part_count = N_GX * N_GY
    entity = entity_table.reshape(N_GX, N_GY, ROWS, D)
    buckets = ((1, 1), (0, 1), (1, -1))
    rel_total = jnp.zeros((REL, D, D), jnp.float32)
    for turn_index in range(ROUNDS):
        axis_number, offset = buckets[turn_index % 3]
        partner = jnp.roll(entity, offset, axis=axis_number)
        group_ids = rel_ids[turn_index].reshape(part_count, GROUPS)
        sources = edge_src[turn_index].reshape(part_count, EDGES_DEV)
        targets = edge_dst[turn_index].reshape(part_count, EDGES_DEV)

        def visit(carry, item):
            src_rows, dst_rows, ids_row, src_row, dst_row = item
            src_grad, dst_grad, rel_part = bucket_terms(src_rows, dst_rows, relations, ids_row, src_row, dst_row)
            return (carry + rel_part, (src_grad, dst_grad))
        rel_total, grads = lax.scan(visit, rel_total, (entity.reshape(part_count, ROWS, D), partner.reshape(part_count, ROWS, D), group_ids, sources, targets))
        src_grad, dst_grad = grads
        returned = jnp.roll(dst_grad.reshape(N_GX, N_GY, ROWS, D), -offset, axis=axis_number)
        entity = entity - learn_rate * (src_grad.reshape(N_GX, N_GY, ROWS, D) + returned)
    new_table = entity.reshape(ROWS * part_count, D)
    rel_grad = rel_total / math.sqrt(ROUNDS * part_count)
    return (new_table, rel_grad)
```

```python
import functools
import math

import jax
import jax.numpy as jnp
from jax import lax
from jax.experimental import pallas as pl
from jax.experimental.pallas import tpu as pltpu
from jax.sharding import PartitionSpec as P

learn_rate = 0.5
MESH = pl.DeviceIdType.MESH
f32, bf16 = jnp.float32, jnp.bfloat16
buckets = (("gy", 1), ("gx", 1), ("gy", -1))
lanes = 128
least_rows = 16


def matmul(left, right, left_dim, right_dim):
    return lax.dot_general(
        left, right, (((left_dim,), (right_dim,)), ((), ())), preferred_element_type=f32
    )


def chunk_of(count):
    for chunk in (1024, 512, 256, 128):
        if count % chunk == 0:
            return chunk
    return count


def kernel(
    na, nb, divisor, ids, x_in, rel_in, src, dst, base_out, ret_out, rel_out,
    x, xb, fetched, mapped, grads, returned, counts, relb, rel_acc, pieces,
    part_x, part_sum, part_y, gathered,
    fetch_send, fetch_recv, ret_send, ret_recv, rsx_send, rsx_recv, rsy_send, rsy_recv,
    agy_send, agy_recv, agx_send, agx_recv,
):
    a, b = lax.axis_index("gx"), lax.axis_index("gy")
    rounds, groups = ids.shape
    rows, feature = x_in.shape
    kinds = rel_in.shape[0]
    block = rows // groups
    edges = src.shape[1]
    scaling = 1.0 / math.sqrt(rows)
    flat_rows = gathered.shape[0]
    rows_a = flat_rows // na
    owners = min(nb, rows_a // least_rows)
    rows_b = rows_a // owners
    half = kinds * feature

    def owning(position):
        if owners == nb:
            return lambda body: body()
        return pl.when(position < owners)

    def at_x(step):
        return lax.rem(a + step + na, na)

    def at_y(step):
        return lax.rem(b + step + nb, nb)

    barrier = pltpu.get_barrier_semaphore()
    for i in range(1, na):
        pl.semaphore_signal(barrier, inc=1, device_id=(at_x(i), b), device_id_type=MESH)
    for i in range(1, nb):
        pl.semaphore_signal(barrier, inc=1, device_id=(a, at_y(i)), device_id_type=MESH)
    x[...] = x_in[...]
    xb[0] = x_in[...].astype(bf16)
    pl.semaphore_wait(barrier, na + nb - 2)

    def ring(turn, back):
        axis, offset = buckets[turn % len(buckets)]
        step = -offset if back else offset
        return (at_x(step), b) if axis == "gx" else (a, at_y(step))

    def fetch(turn):
        return pltpu.make_async_remote_copy(
            src_ref=xb.at[turn], dst_ref=fetched.at[turn],
            send_sem=fetch_send.at[turn], recv_sem=fetch_recv.at[turn],
            device_id=ring(turn, False), device_id_type=MESH,
        )

    def give_back(turn):
        return pltpu.make_async_remote_copy(
            src_ref=grads.at[turn], dst_ref=returned.at[turn],
            send_sem=ret_send.at[turn], recv_sem=ret_recv.at[turn],
            device_id=ring(turn, True), device_id_type=MESH,
        )

    def count(turn):
        chunk = chunk_of(edges)
        spots = lax.broadcasted_iota(jnp.int32, (rows, chunk), 0).astype(f32).astype(bf16)
        one, zero = jnp.ones((), bf16), jnp.zeros((), bf16)
        total = None
        for start in range(0, edges, chunk):
            s = src[turn : turn + 1, start : start + chunk].astype(f32).astype(bf16)
            t = dst[turn : turn + 1, start : start + chunk].astype(f32).astype(bf16)
            s_hot = jnp.where(spots == s, one, zero)
            t_hot = jnp.where(spots == t, one, zero)
            term = matmul(s_hot, t_hot, 1, 1)
            total = term if total is None else total + term
        counts[...] = total

    fetch(0).start()
    for kind in range(kinds):
        relb[kind] = rel_in[kind].astype(bf16)
    count(0)

    for turn in range(rounds):
        last = turn == rounds - 1
        if turn > 0:
            xb[turn] = x[...].astype(bf16)
            fetch(turn).start()
        for g in range(groups):
            span = slice(g * block, (g + 1) * block)
            mapped[span, :] = matmul(xb[turn, span, :], relb[ids[turn, g]], 1, 0).astype(bf16)
        turned = xb[turn].T
        column = lax.broadcasted_iota(jnp.int32, (1, rows), 1) // block
        kind_of = jnp.zeros((1, rows), jnp.int32)
        for g in range(groups):
            kind_of = jnp.where(column == g, ids[turn, g], kind_of)

        fetch(turn).wait_recv()
        their = fetched[turn]
        scores = matmul(mapped[...], their, 1, 1)
        slopes = ((0.5 * jnp.tanh(0.5 * scores) + 0.5 - counts[...]) * scaling).astype(bf16)

        def pull():
            return matmul(slopes, their, 1, 0).astype(bf16)

        def return_gradient():
            grads[turn] = matmul(slopes, mapped[...], 0, 0).astype(bf16)
            give_back(turn).start()

        def relation_term():
            for kind in range(kinds):
                chosen = turned * (kind_of == kind).astype(f32).astype(bf16)
                term = matmul(chosen, pulled, 1, 0)
                place = slice(kind * feature, (kind + 1) * feature)
                if turn > 0:
                    term = term + rel_acc[place, :]
                rel_acc[place, :] = term / divisor if last else term

        if last:
            pulled = pull()
            relation_term()
            for part in range(feature // lanes):
                pieces[part * half : (part + 1) * half, :] = rel_acc[
                    :, part * lanes : (part + 1) * lanes
                ].astype(bf16)
        else:
            return_gradient()
            pulled = pull()

        if last:
            def scatter_x(i):
                return pltpu.make_async_remote_copy(
                    src_ref=pieces.at[pl.ds(pl.multiple_of(at_x(i) * rows_a, rows_a), rows_a), :],
                    dst_ref=part_x.at[i],
                    send_sem=rsx_send.at[i], recv_sem=rsx_recv.at[i],
                    device_id=(at_x(i), b), device_id_type=MESH,
                )

            for i in range(1, na):
                scatter_x(i).start()
            return_gradient()

        for g in range(groups):
            span = slice(g * block, (g + 1) * block)
            pull_g = pulled[span, :]
            x[span, :] = x[span, :] - learn_rate * matmul(pull_g, relb[ids[turn, g]], 1, 1)
        if not last:
            relation_term()
            count(turn + 1)
            give_back(turn).wait_recv()
            x[...] = x[...] - learn_rate * returned[turn].astype(f32)

    base_out[...] = x[...]

    def scatter_y(i):
        return pltpu.make_async_remote_copy(
            src_ref=part_sum.at[pl.ds(pl.multiple_of(at_y(i) * rows_b, rows_b), rows_b), :],
            dst_ref=part_y.at[i],
            send_sem=rsy_send.at[i], recv_sem=rsy_recv.at[i],
            device_id=(a, at_y(i)), device_id_type=MESH,
        )

    def spot(x_pos, y_pos):
        return gathered.at[
            pl.ds(pl.multiple_of(x_pos * rows_a + y_pos * rows_b, rows_b), rows_b), :
        ]

    def gather_y(i, y_pos):
        return pltpu.make_async_remote_copy(
            src_ref=spot(a, y_pos), dst_ref=spot(a, y_pos),
            send_sem=agy_send.at[i], recv_sem=agy_recv.at[i],
            device_id=(a, at_y(i)), device_id_type=MESH,
        )

    def gather_x(j, i, x_pos, y_pos):
        return pltpu.make_async_remote_copy(
            src_ref=spot(x_pos, y_pos), dst_ref=spot(x_pos, y_pos),
            send_sem=agx_send.at[j, i], recv_sem=agx_recv.at[j, i],
            device_id=(at_x(j), b), device_id_type=MESH,
        )

    own = pieces[pl.ds(pl.multiple_of(a * rows_a, rows_a), rows_a), :].astype(f32)
    for i in range(1, na):
        scatter_x(i).wait_recv()
        own = own + part_x[i].astype(f32)
    part_sum[...] = own.astype(bf16)
    for i in range(1, nb):
        @owning(at_y(i))
        def _():
            scatter_y(i).start()

    @owning(b)
    def _():
        mine = part_sum[pl.ds(pl.multiple_of(b * rows_b, rows_b), rows_b), :].astype(f32)
        for i in range(1, nb):
            scatter_y(i).wait_recv()
            mine = mine + part_y[i].astype(f32)
        gathered[pl.ds(pl.multiple_of(a * rows_a + b * rows_b, rows_b), rows_b), :] = mine.astype(bf16)
        for i in range(1, nb):
            gather_y(i, b).start()
        for j in range(1, na):
            gather_x(j, 0, a, b).start()

    for i in range(1, nb):
        @owning(at_y(-i))
        def _():
            gather_y(i, at_y(-i)).wait_recv()
            for j in range(1, na):
                gather_x(j, i, a, at_y(-i)).start()

    give_back(rounds - 1).wait_recv()
    ret_out[...] = returned[rounds - 1]
    for i in range(nb):
        @owning(at_y(-i))
        def _():
            for j in range(1, na):
                gather_x(j, i, at_x(-j), at_y(-i)).wait_recv()
    rel_out[...] = gathered[...]

    for turn in range(rounds):
        fetch(turn).wait_send()
        give_back(turn).wait_send()
    for i in range(1, na):
        scatter_x(i).wait_send()
    for i in range(1, nb):
        @owning(at_y(i))
        def _():
            scatter_y(i).wait_send()

        @owning(b)
        def _():
            gather_y(i, b).wait_send()
    for i in range(nb):
        @owning(at_y(-i))
        def _():
            for j in range(1, na):
                gather_x(j, i, a, at_y(-i)).wait_send()


def shards(na, nb, entity, relations, rel_ids, edge_src, edge_dst):
    rows, feature = entity.shape
    rounds, groups = rel_ids.shape
    kinds = relations.shape[0]
    flat = kinds * feature * feature // lanes
    rows_a = flat // na
    rows_b = rows_a // min(nb, rows_a // least_rows)
    divisor = math.sqrt(rounds * na * nb)
    dma = pltpu.SemaphoreType.DMA
    in_vmem = pl.BlockSpec(memory_space=pltpu.VMEM)
    base, ret, rel = pl.pallas_call(
        functools.partial(kernel, na, nb, divisor),
        out_shape=(
            jax.ShapeDtypeStruct((rows, feature), f32),
            jax.ShapeDtypeStruct((rows, feature), bf16),
            jax.ShapeDtypeStruct((flat, lanes), bf16),
        ),
        in_specs=[pl.BlockSpec(memory_space=pltpu.SMEM)] + [in_vmem] * 4,
        out_specs=(in_vmem,) * 3,
        scratch_shapes=[
            pltpu.VMEM((rows, feature), f32),
            pltpu.VMEM((rounds, rows, feature), bf16),
            pltpu.VMEM((rounds, rows, feature), bf16),
            pltpu.VMEM((rows, feature), bf16),
            pltpu.VMEM((rounds, rows, feature), bf16),
            pltpu.VMEM((rounds, rows, feature), bf16),
            pltpu.VMEM((rows, rows), f32),
            pltpu.VMEM((kinds, feature, feature), bf16),
            pltpu.VMEM((kinds * feature, feature), f32),
            pltpu.VMEM((flat, lanes), bf16),
            pltpu.VMEM((na, rows_a, lanes), bf16),
            pltpu.VMEM((rows_a, lanes), bf16),
            pltpu.VMEM((nb, rows_b, lanes), bf16),
            pltpu.VMEM((flat, lanes), bf16),
            dma((rounds,)), dma((rounds,)), dma((rounds,)), dma((rounds,)),
            dma((na,)), dma((na,)), dma((nb,)), dma((nb,)),
            dma((nb,)), dma((nb,)), dma((na, nb)), dma((na, nb)),
        ],
        compiler_params=pltpu.CompilerParams(
            collective_id=0, has_side_effects=True, vmem_limit_bytes=40 * 1024 * 1024
        ),
    )(rel_ids, entity, relations, edge_src, edge_dst)
    table = base - learn_rate * ret.astype(f32)
    parts = feature // lanes
    rel = rel.reshape(parts, kinds, feature, lanes).transpose(1, 2, 0, 3)
    return table, rel.reshape(kinds, feature, feature).astype(f32)


def solution(mesh):
    return jax.shard_map(
        functools.partial(shards, mesh.shape["gx"], mesh.shape["gy"]),
        mesh=mesh,
        in_specs=(
            P(("gx", "gy"), None),
            P(),
            P(None, ("gx", "gy")),
            P(None, ("gx", "gy")),
            P(None, ("gx", "gy")),
        ),
        out_specs=(P(("gx", "gy"), None), P()),
        check_vma=False,
    )
```

```python
import functools
import math

import jax
import jax.numpy as jnp
from jax import lax
from jax.experimental import pallas as pl
from jax.experimental.pallas import tpu as pltpu
from jax.sharding import PartitionSpec as P

learn_rate = 0.5
MESH = pl.DeviceIdType.MESH
f32, bf16 = jnp.float32, jnp.bfloat16
buckets = (("gy", 1), ("gx", 1), ("gy", -1))
lanes = 128
least_rows = 16


def matmul(left, right, left_dim, right_dim):
    return lax.dot_general(
        left, right, (((left_dim,), (right_dim,)), ((), ())), preferred_element_type=f32
    )


def chunk_of(count):
    for chunk in (1024, 512, 256, 128):
        if count % chunk == 0:
            return chunk
    return count


def kernel(
    na, nb, divisor, ids_in, x_in, rel_in, src_in, dst_in, base_out, ret_out, rel_out,
    ids, rel, src, dst,
    x, xb, fetched, mapped, grads, returned, counts, relb, rel_acc, pieces,
    part_x, part_sum, part_y, gathered,
    load_sem, store_sem,
    fetch_send, fetch_recv, ret_send, ret_recv, rsx_send, rsx_recv, rsy_send, rsy_recv,
    agy_send, agy_recv, agx_send, agx_recv,
):
    a, b = lax.axis_index("gx"), lax.axis_index("gy")
    rounds, groups = ids.shape
    rows, feature = x.shape
    kinds = rel.shape[0]
    block = rows // groups
    edges = src.shape[1]
    scaling = 1.0 / math.sqrt(rows)
    parts = fetch_send.shape[1]
    rows_p = rows // parts
    flat_k = gathered.shape[0] // kinds
    rows_a = flat_k // na
    owners = min(nb, rows_a // least_rows)
    rows_b = rows_a // owners

    loads = [
        pltpu.make_async_copy(source, target, load_sem.at[i])
        for i, (source, target) in enumerate(
            ((x_in, x), (src_in, src), (dst_in, dst), (ids_in, ids), (rel_in, rel))
        )
    ]
    for load in loads:
        load.start()

    def owning(position):
        if owners == nb:
            return lambda body: body()
        return pl.when(position < owners)

    def at_x(step):
        return lax.rem(a + step + na, na)

    def at_y(step):
        return lax.rem(b + step + nb, nb)

    barrier = pltpu.get_barrier_semaphore()
    for i in range(1, na):
        pl.semaphore_signal(barrier, inc=1, device_id=(at_x(i), b), device_id_type=MESH)
    for i in range(1, nb):
        pl.semaphore_signal(barrier, inc=1, device_id=(a, at_y(i)), device_id_type=MESH)

    def ring(turn, back):
        axis, offset = buckets[turn % len(buckets)]
        step = -offset if back else offset
        return (at_x(step), b) if axis == "gx" else (a, at_y(step))

    def part_of(c):
        return slice(c * rows_p, (c + 1) * rows_p)

    def fetch(turn, c):
        here = pl.ds(c * rows_p, rows_p)
        return pltpu.make_async_remote_copy(
            src_ref=xb.at[turn, here, :], dst_ref=fetched.at[turn, here, :],
            send_sem=fetch_send.at[turn, c], recv_sem=fetch_recv.at[turn, c],
            device_id=ring(turn, False), device_id_type=MESH,
        )

    def give_back(turn, c):
        here = pl.ds(c * rows_p, rows_p)
        return pltpu.make_async_remote_copy(
            src_ref=grads.at[turn, here, :], dst_ref=returned.at[turn, here, :],
            send_sem=ret_send.at[turn, c], recv_sem=ret_recv.at[turn, c],
            device_id=ring(turn, True), device_id_type=MESH,
        )

    def count(turn):
        chunk = chunk_of(edges)
        spots = lax.broadcasted_iota(jnp.int32, (rows, chunk), 0).astype(f32).astype(bf16)
        one, zero = jnp.ones((), bf16), jnp.zeros((), bf16)
        total = None
        for start in range(0, edges, chunk):
            s = src[turn : turn + 1, start : start + chunk].astype(f32).astype(bf16)
            t = dst[turn : turn + 1, start : start + chunk].astype(f32).astype(bf16)
            s_hot = jnp.where(spots == s, one, zero)
            t_hot = jnp.where(spots == t, one, zero)
            term = matmul(s_hot, t_hot, 1, 1)
            total = term if total is None else total + term
        counts[...] = total

    def scatter_x(k, i):
        return pltpu.make_async_remote_copy(
            src_ref=pieces.at[pl.ds(pl.multiple_of(k * flat_k + at_x(i) * rows_a, rows_a), rows_a), :],
            dst_ref=part_x.at[k, i],
            send_sem=rsx_send.at[k, i], recv_sem=rsx_recv.at[k, i],
            device_id=(at_x(i), b), device_id_type=MESH,
        )

    def scatter_y(k, i):
        return pltpu.make_async_remote_copy(
            src_ref=part_sum.at[k, pl.ds(pl.multiple_of(at_y(i) * rows_b, rows_b), rows_b), :],
            dst_ref=part_y.at[k, i],
            send_sem=rsy_send.at[k, i], recv_sem=rsy_recv.at[k, i],
            device_id=(a, at_y(i)), device_id_type=MESH,
        )

    def spot(k, y_pos):
        start = k * flat_k + a * rows_a + y_pos * rows_b
        return pl.ds(pl.multiple_of(start, rows_b), rows_b)

    def gather_y(k, i, y_pos):
        return pltpu.make_async_remote_copy(
            src_ref=gathered.at[spot(k, y_pos), :], dst_ref=gathered.at[spot(k, y_pos), :],
            send_sem=agy_send.at[k, i], recv_sem=agy_recv.at[k, i],
            device_id=(a, at_y(i)), device_id_type=MESH,
        )

    def gather_x(k, i, x_pos):
        here = pl.ds(pl.multiple_of(k * flat_k + x_pos * rows_a, rows_a), rows_a)
        return pltpu.make_async_remote_copy(
            src_ref=gathered.at[here, :], dst_ref=gathered.at[here, :],
            send_sem=agx_send.at[k, i], recv_sem=agx_recv.at[k, i],
            device_id=(at_x(i), b), device_id_type=MESH,
        )

    loads[0].wait()
    xb[0] = x[...].astype(bf16)
    pl.semaphore_wait(barrier, na + nb - 2)
    for c in range(parts):
        fetch(0, c).start()
    for load in loads[1:]:
        load.wait()
    for kind in range(kinds):
        relb[kind] = rel[kind].astype(bf16)

    def map_rows(turn):
        for g in range(groups):
            span = slice(g * block, (g + 1) * block)
            mapped[span, :] = matmul(xb[turn, span, :], relb[ids[turn, g]], 1, 0).astype(bf16)

    map_rows(0)
    count(0)

    for turn in range(rounds):
        last = turn == rounds - 1
        if turn > 0:
            map_rows(turn)
        turned = xb[turn].T
        column = lax.broadcasted_iota(jnp.int32, (1, rows), 1) // block
        kind_of = jnp.zeros((1, rows), jnp.int32)
        for g in range(groups):
            kind_of = jnp.where(column == g, ids[turn, g], kind_of)
        here_b = mapped[...]

        slopes = []
        total = None
        for c in range(parts):
            fetch(turn, c).wait_recv()
            their = fetched[turn, part_of(c), :]
            scores = matmul(here_b, their, 1, 1)
            slope = (
                (0.5 * jnp.tanh(0.5 * scores) + 0.5 - counts[:, part_of(c)]) * scaling
            ).astype(bf16)
            slopes.append(slope)
            if not last:
                grads[turn, part_of(c), :] = matmul(slope, here_b, 0, 0).astype(bf16)
                give_back(turn, c).start()
            term = matmul(slope, their, 1, 0)
            total = term if total is None else total + term
        pulled = total.astype(bf16)

        def relation_term():
            for kind in range(kinds):
                chosen = turned * (kind_of == kind).astype(f32).astype(bf16)
                term = matmul(chosen, pulled, 1, 0)
                place = slice(kind * feature, (kind + 1) * feature)
                if turn > 0:
                    term = term + rel_acc[place, :]
                if not last:
                    rel_acc[place, :] = term
                    continue
                term = (term * (1.0 / divisor)).astype(bf16)
                for side in range(feature // lanes):
                    start = kind * flat_k + side * feature
                    pieces[start : start + feature, :] = term[:, side * lanes : (side + 1) * lanes]
                for i in range(1, na):
                    scatter_x(kind, i).start()

        if last:
            relation_term()
            for c in range(parts):
                grads[turn, part_of(c), :] = matmul(slopes[c], here_b, 0, 0).astype(bf16)
                give_back(turn, c).start()
        for g in range(groups):
            span = slice(g * block, (g + 1) * block)
            x[span, :] = x[span, :] - learn_rate * matmul(pulled[span, :], relb[ids[turn, g]], 1, 1)
        if not last:
            relation_term()
            count(turn + 1)
            for c in range(parts):
                give_back(turn, c).wait_recv()
                moved = x[part_of(c), :] - learn_rate * returned[turn, part_of(c), :].astype(f32)
                x[part_of(c), :] = moved
                xb[turn + 1, part_of(c), :] = moved.astype(bf16)
                fetch(turn + 1, c).start()

    store_base = pltpu.make_async_copy(x, base_out, store_sem.at[0])
    store_base.start()

    def reduce_x(k):
        start = k * flat_k + a * rows_a
        own = pieces[pl.ds(pl.multiple_of(start, rows_a), rows_a), :].astype(f32)
        for i in range(1, na):
            scatter_x(k, i).wait_recv()
            own = own + part_x[k, i].astype(f32)
        part_sum[k] = own.astype(bf16)
        for i in range(1, nb):
            @owning(at_y(i))
            def _():
                scatter_y(k, i).start()

    def reduce_y(k):
        @owning(b)
        def _():
            mine = part_sum[k, pl.ds(pl.multiple_of(b * rows_b, rows_b), rows_b), :].astype(f32)
            for i in range(1, nb):
                scatter_y(k, i).wait_recv()
                mine = mine + part_y[k, i].astype(f32)
            gathered[spot(k, b), :] = mine.astype(bf16)
            for i in range(1, nb):
                gather_y(k, i, b).start()

    def spread(k):
        for i in range(1, nb):
            @owning(at_y(-i))
            def _():
                gather_y(k, i, at_y(-i)).wait_recv()
        for i in range(1, na):
            gather_x(k, i, a).start()

    for step in range(kinds + 2):
        if step < kinds:
            reduce_x(step)
        if 0 <= step - 1 < kinds:
            reduce_y(step - 1)
        if 0 <= step - 2:
            spread(step - 2)

    for c in range(parts):
        give_back(rounds - 1, c).wait_recv()
    store_ret = pltpu.make_async_copy(returned.at[rounds - 1], ret_out, store_sem.at[1])
    store_ret.start()
    stores = [store_base, store_ret]
    for k in range(kinds):
        for i in range(1, na):
            gather_x(k, i, at_x(-i)).wait_recv()
        here = pl.ds(k * flat_k, flat_k)
        store = pltpu.make_async_copy(gathered.at[here, :], rel_out.at[here, :], store_sem.at[2 + k])
        store.start()
        stores.append(store)

    for turn in range(rounds):
        for c in range(parts):
            fetch(turn, c).wait_send()
            give_back(turn, c).wait_send()
    for k in range(kinds):
        for i in range(1, na):
            scatter_x(k, i).wait_send()
            gather_x(k, i, a).wait_send()
        for i in range(1, nb):
            @owning(at_y(i))
            def _():
                scatter_y(k, i).wait_send()

            @owning(b)
            def _():
                gather_y(k, i, b).wait_send()
    for store in stores:
        store.wait()


def shards(na, nb, entity, relations, rel_ids, edge_src, edge_dst):
    rows, feature = entity.shape
    rounds, groups = rel_ids.shape
    kinds = relations.shape[0]
    parts = 2
    flat = kinds * feature * feature // lanes
    rows_a = flat // kinds // na
    rows_b = rows_a // min(nb, rows_a // least_rows)
    divisor = math.sqrt(rounds * na * nb)
    dma = pltpu.SemaphoreType.DMA
    in_hbm = pl.BlockSpec(memory_space=pltpu.HBM)
    base, ret, rel = pl.pallas_call(
        functools.partial(kernel, na, nb, divisor),
        out_shape=(
            jax.ShapeDtypeStruct((rows, feature), f32),
            jax.ShapeDtypeStruct((rows, feature), bf16),
            jax.ShapeDtypeStruct((flat, lanes), bf16),
        ),
        in_specs=[in_hbm] * 5,
        out_specs=(in_hbm,) * 3,
        scratch_shapes=[
            pltpu.SMEM(rel_ids.shape, jnp.int32),
            pltpu.VMEM(relations.shape, f32),
            pltpu.VMEM(edge_src.shape, jnp.int32),
            pltpu.VMEM(edge_dst.shape, jnp.int32),
            pltpu.VMEM((rows, feature), f32),
            pltpu.VMEM((rounds, rows, feature), bf16),
            pltpu.VMEM((rounds, rows, feature), bf16),
            pltpu.VMEM((rows, feature), bf16),
            pltpu.VMEM((rounds, rows, feature), bf16),
            pltpu.VMEM((rounds, rows, feature), bf16),
            pltpu.VMEM((rows, rows), f32),
            pltpu.VMEM((kinds, feature, feature), bf16),
            pltpu.VMEM((kinds * feature, feature), f32),
            pltpu.VMEM((flat, lanes), bf16),
            pltpu.VMEM((kinds, na, rows_a, lanes), bf16),
            pltpu.VMEM((kinds, rows_a, lanes), bf16),
            pltpu.VMEM((kinds, nb, rows_b, lanes), bf16),
            pltpu.VMEM((flat, lanes), bf16),
            dma((5,)), dma((2 + kinds,)),
            dma((rounds, parts)), dma((rounds, parts)), dma((rounds, parts)), dma((rounds, parts)),
            dma((kinds, na)), dma((kinds, na)), dma((kinds, nb)), dma((kinds, nb)),
            dma((kinds, nb)), dma((kinds, nb)), dma((kinds, na)), dma((kinds, na)),
        ],
        compiler_params=pltpu.CompilerParams(
            collective_id=0, has_side_effects=True, vmem_limit_bytes=40 * 1024 * 1024
        ),
    )(rel_ids, entity, relations, edge_src, edge_dst)
    table = base - learn_rate * ret.astype(f32)
    sides = feature // lanes
    rel = rel.reshape(kinds, sides, feature, lanes).transpose(0, 2, 1, 3)
    return table, rel.reshape(kinds, feature, feature).astype(f32)


def solution(mesh):
    return jax.shard_map(
        functools.partial(shards, mesh.shape["gx"], mesh.shape["gy"]),
        mesh=mesh,
        in_specs=(
            P(("gx", "gy"), None),
            P(),
            P(None, ("gx", "gy")),
            P(None, ("gx", "gy")),
            P(None, ("gx", "gy")),
        ),
        out_specs=(P(("gx", "gy"), None), P()),
        check_vma=False,
    )
```

```python
import functools
import math

import jax
import jax.numpy as jnp
from jax import lax
from jax.experimental import pallas as pl
from jax.experimental.pallas import tpu as pltpu
from jax.sharding import PartitionSpec as P

learn_rate = 0.5
MESH = pl.DeviceIdType.MESH
f32, bf16 = jnp.float32, jnp.bfloat16
buckets = (("gy", 1), ("gx", 1), ("gy", -1))
lanes = 128
least_rows = 16


def matmul(left, right, left_dim, right_dim):
    return lax.dot_general(
        left, right, (((left_dim,), (right_dim,)), ((), ())), preferred_element_type=f32
    )


def chunk_of(count):
    for chunk in (1024, 512, 256, 128):
        if count % chunk == 0:
            return chunk
    return count


def kernel(
    na, nb, divisor, ids_in, x_in, rel_in, src_in, dst_in, base_out, ret_out, rel_out,
    ids, rel, src, dst,
    x, xb, fetched, mapped, grads, returned, counts, relb, rel_acc, pieces,
    part_x, part_sum, part_y, gathered,
    load_sem, store_sem,
    fetch_send, fetch_recv, ret_send, ret_recv, rsx_send, rsx_recv, rsy_send, rsy_recv,
    agy_send, agy_recv, agx_send, agx_recv,
):
    a, b = lax.axis_index("gx"), lax.axis_index("gy")
    rounds, groups = ids.shape
    rows, feature = x.shape
    kinds = rel.shape[0]
    block = rows // groups
    edges = src.shape[1]
    scaling = 1.0 / math.sqrt(rows)
    parts = fetch_recv.shape[1]
    rows_p = rows // parts
    chunks = part_x.shape[0]
    flat = gathered.shape[0]
    flat_k = flat // chunks
    rows_a = flat_k // na
    owners = min(nb, rows_a // least_rows)
    rows_b = rows_a // owners

    loads = [
        pltpu.make_async_copy(source, target, load_sem.at[i])
        for i, (source, target) in enumerate(
            ((x_in, x), (src_in, src), (dst_in, dst), (ids_in, ids), (rel_in, rel))
        )
    ]
    for load in loads:
        load.start()

    def owning(position):
        if owners == nb:
            return lambda body: body()
        return pl.when(position < owners)

    def at_x(step):
        return lax.rem(a + step + na, na)

    def at_y(step):
        return lax.rem(b + step + nb, nb)

    barrier = pltpu.get_barrier_semaphore()
    for i in range(1, na):
        pl.semaphore_signal(barrier, inc=1, device_id=(at_x(i), b), device_id_type=MESH)
    for i in range(1, nb):
        pl.semaphore_signal(barrier, inc=1, device_id=(a, at_y(i)), device_id_type=MESH)

    def ring(turn, back):
        axis, offset = buckets[turn % len(buckets)]
        step = -offset if back else offset
        return (at_x(step), b) if axis == "gx" else (a, at_y(step))

    def part_of(c):
        return slice(c * rows_p, (c + 1) * rows_p)

    def fetch(turn, c):
        here = pl.ds(c * rows_p, rows_p)
        return pltpu.make_async_remote_copy(
            src_ref=xb.at[turn, here, :], dst_ref=fetched.at[turn, here, :],
            send_sem=fetch_send.at[0], recv_sem=fetch_recv.at[turn, c],
            device_id=ring(turn, False), device_id_type=MESH,
        )

    def give_back(turn, c):
        here = pl.ds(c * rows_p, rows_p)
        return pltpu.make_async_remote_copy(
            src_ref=grads.at[turn, here, :], dst_ref=returned.at[turn, here, :],
            send_sem=ret_send.at[0], recv_sem=ret_recv.at[turn, c],
            device_id=ring(turn, True), device_id_type=MESH,
        )

    def await_rows(count, sem):
        held = gathered.at[pl.ds(0, count), :]
        pltpu.make_async_copy(held, held, sem).wait()

    def await_owners(weight, sem):
        if owners == nb:
            await_rows((nb - 1) * weight, sem)
            return

        @pl.when(b >= owners)
        def _():
            await_rows(owners * weight, sem)

        if owners > 1:
            @pl.when(b < owners)
            def _():
                await_rows((owners - 1) * weight, sem)

    def count(turn, section, sections):
        chunk = chunk_of(edges)
        spots = lax.broadcasted_iota(jnp.int32, (rows, chunk), 0).astype(f32).astype(bf16)
        one, zero = jnp.ones((), bf16), jnp.zeros((), bf16)
        total = None
        starts = range(0, edges, chunk)
        size = -(-len(starts) // sections)
        for start in starts[section * size : (section + 1) * size]:
            s = src[turn : turn + 1, start : start + chunk].astype(f32).astype(bf16)
            t = dst[turn : turn + 1, start : start + chunk].astype(f32).astype(bf16)
            s_hot = jnp.where(spots == s, one, zero)
            t_hot = jnp.where(spots == t, one, zero)
            term = matmul(s_hot, t_hot, 1, 1)
            total = term if total is None else total + term
        if total is not None:
            counts[...] = counts[...] + total if section > 0 else total

    def scatter_x(k, i):
        return pltpu.make_async_remote_copy(
            src_ref=pieces.at[pl.ds(pl.multiple_of(k * flat_k + at_x(i) * rows_a, rows_a), rows_a), :],
            dst_ref=part_x.at[k, i],
            send_sem=rsx_send.at[0], recv_sem=rsx_recv.at[k],
            device_id=(at_x(i), b), device_id_type=MESH,
        )

    def scatter_y(k, i):
        return pltpu.make_async_remote_copy(
            src_ref=part_sum.at[k, pl.ds(pl.multiple_of(at_y(i) * rows_b, rows_b), rows_b), :],
            dst_ref=part_y.at[k, i],
            send_sem=rsy_send.at[0], recv_sem=rsy_recv.at[k],
            device_id=(a, at_y(i)), device_id_type=MESH,
        )

    def spot(k, y_pos):
        start = k * flat_k + a * rows_a + y_pos * rows_b
        return pl.ds(pl.multiple_of(start, rows_b), rows_b)

    def gather_y(k, i, y_pos):
        return pltpu.make_async_remote_copy(
            src_ref=gathered.at[spot(k, y_pos), :], dst_ref=gathered.at[spot(k, y_pos), :],
            send_sem=agy_send.at[0], recv_sem=agy_recv.at[k],
            device_id=(a, at_y(i)), device_id_type=MESH,
        )

    def gather_x(k, i, x_pos):
        here = pl.ds(pl.multiple_of(k * flat_k + x_pos * rows_a, rows_a), rows_a)
        return pltpu.make_async_remote_copy(
            src_ref=gathered.at[here, :], dst_ref=gathered.at[here, :],
            send_sem=agx_send.at[0], recv_sem=agx_recv.at[k],
            device_id=(at_x(i), b), device_id_type=MESH,
        )

    loads[0].wait()
    xb[0] = x[...].astype(bf16)
    pl.semaphore_wait(barrier, na + nb - 2)
    for c in range(parts):
        fetch(0, c).start()
    for load in loads[1:]:
        load.wait()
    for kind in range(kinds):
        relb[kind] = rel[kind].astype(bf16)

    def map_rows(turn):
        for g in range(groups):
            span = slice(g * block, (g + 1) * block)
            mapped[span, :] = matmul(xb[turn, span, :], relb[ids[turn, g]], 1, 0).astype(bf16)

    map_rows(0)
    count(0, 0, 1)

    for turn in range(rounds):
        last = turn == rounds - 1
        if turn > 0:
            map_rows(turn)
            relation_term()
            count(turn, 1, 2)
        turned = xb[turn].T
        column = lax.broadcasted_iota(jnp.int32, (1, rows), 1) // block
        kind_of = jnp.zeros((1, rows), jnp.int32)
        for g in range(groups):
            kind_of = jnp.where(column == g, ids[turn, g], kind_of)
        here_b = mapped[...]

        slopes = []
        total = None
        for c in range(parts):
            fetch(turn, c).wait_recv()
            their = fetched[turn, part_of(c), :]
            scores = matmul(here_b, their, 1, 1)
            slope = (
                (0.5 * jnp.tanh(0.5 * scores) + 0.5 - counts[:, part_of(c)]) * scaling
            ).astype(bf16)
            slopes.append(slope)
            if not last:
                grads[turn, part_of(c), :] = matmul(slope, here_b, 0, 0).astype(bf16)
                give_back(turn, c).start()
            term = matmul(slope, their, 1, 0)
            total = term if total is None else total + term
        pulled = total.astype(bf16)

        def relation_term(turn=turn, last=last, turned=turned, kind_of=kind_of, pulled=pulled):
            for kind in range(kinds):
                chosen = turned * (kind_of == kind).astype(f32).astype(bf16)
                term = matmul(chosen, pulled, 1, 0)
                place = slice(kind * feature, (kind + 1) * feature)
                if turn > 0:
                    term = term + rel_acc[place, :]
                if not last:
                    rel_acc[place, :] = term
                    continue
                term = (term * (1.0 / divisor)).astype(bf16)
                for side in range(feature // lanes):
                    start = kind * (flat // kinds) + side * feature
                    pieces[start : start + feature, :] = term[:, side * lanes : (side + 1) * lanes]
                if (kind + 1) % (kinds // chunks) == 0:
                    for i in range(1, na):
                        scatter_x(kind // (kinds // chunks), i).start()

        if last:
            relation_term()
            for c in range(parts):
                grads[turn, part_of(c), :] = matmul(slopes[c], here_b, 0, 0).astype(bf16)
                give_back(turn, c).start()
        for g in range(groups):
            span = slice(g * block, (g + 1) * block)
            x[span, :] = x[span, :] - learn_rate * matmul(pulled[span, :], relb[ids[turn, g]], 1, 1)
        if not last:
            count(turn + 1, 0, 2)
            for c in range(parts):
                give_back(turn, c).wait_recv()
                moved = x[part_of(c), :] - learn_rate * returned[turn, part_of(c), :].astype(f32)
                x[part_of(c), :] = moved
                xb[turn + 1, part_of(c), :] = moved.astype(bf16)
                fetch(turn + 1, c).start()

    store_base = pltpu.make_async_copy(x, base_out, store_sem.at[0])
    store_base.start()

    def reduce_x(k):
        start = k * flat_k + a * rows_a
        own = pieces[pl.ds(pl.multiple_of(start, rows_a), rows_a), :].astype(f32)
        await_rows((na - 1) * rows_a, rsx_recv.at[k])
        for i in range(1, na):
            own = own + part_x[k, i].astype(f32)
        part_sum[k] = own.astype(bf16)
        for i in range(1, nb):
            @owning(at_y(i))
            def _():
                scatter_y(k, i).start()

    def reduce_y(k):
        @owning(b)
        def _():
            mine = part_sum[k, pl.ds(pl.multiple_of(b * rows_b, rows_b), rows_b), :].astype(f32)
            await_rows((nb - 1) * rows_b, rsy_recv.at[k])
            for i in range(1, nb):
                mine = mine + part_y[k, i].astype(f32)
            gathered[spot(k, b), :] = mine.astype(bf16)
            for i in range(1, nb):
                gather_y(k, i, b).start()

    def spread(k):
        await_owners(rows_b, agy_recv.at[k])
        for i in range(1, na):
            gather_x(k, i, a).start()

    for step in range(chunks + 2):
        if step < chunks:
            reduce_x(step)
        if 0 <= step - 1 < chunks:
            reduce_y(step - 1)
        if 0 <= step - 2:
            spread(step - 2)

    for c in range(parts):
        give_back(rounds - 1, c).wait_recv()
    store_ret = pltpu.make_async_copy(returned.at[rounds - 1], ret_out, store_sem.at[1])
    store_ret.start()
    stores = [store_base, store_ret]
    for k in range(chunks):
        await_rows((na - 1) * rows_a, agx_recv.at[k])
        here = pl.ds(k * flat_k, flat_k)
        store = pltpu.make_async_copy(gathered.at[here, :], rel_out.at[here, :], store_sem.at[2 + k])
        store.start()
        stores.append(store)

    pltpu.make_async_copy(fetched, fetched, fetch_send.at[0]).wait()
    pltpu.make_async_copy(fetched, fetched, ret_send.at[0]).wait()
    await_rows(chunks * (na - 1) * rows_a, rsx_send.at[0])
    await_rows(chunks * (na - 1) * rows_a, agx_send.at[0])
    await_owners(chunks * rows_b, rsy_send.at[0])

    @owning(b)
    def _():
        await_rows(chunks * (nb - 1) * rows_b, agy_send.at[0])

    for store in stores:
        store.wait()


def shards(na, nb, entity, relations, rel_ids, edge_src, edge_dst):
    rows, feature = entity.shape
    rounds, groups = rel_ids.shape
    kinds = relations.shape[0]
    parts = 2
    chunks = 2 if kinds % 2 == 0 else 1
    flat = kinds * feature * feature // lanes
    rows_a = flat // chunks // na
    rows_b = rows_a // min(nb, rows_a // least_rows)
    divisor = math.sqrt(rounds * na * nb)
    dma = pltpu.SemaphoreType.DMA
    in_hbm = pl.BlockSpec(memory_space=pltpu.HBM)
    base, ret, rel = pl.pallas_call(
        functools.partial(kernel, na, nb, divisor),
        out_shape=(
            jax.ShapeDtypeStruct((rows, feature), f32),
            jax.ShapeDtypeStruct((rows, feature), bf16),
            jax.ShapeDtypeStruct((flat, lanes), bf16),
        ),
        in_specs=[in_hbm] * 5,
        out_specs=(in_hbm,) * 3,
        scratch_shapes=[
            pltpu.SMEM(rel_ids.shape, jnp.int32),
            pltpu.VMEM(relations.shape, f32),
            pltpu.VMEM(edge_src.shape, jnp.int32),
            pltpu.VMEM(edge_dst.shape, jnp.int32),
            pltpu.VMEM((rows, feature), f32),
            pltpu.VMEM((rounds, rows, feature), bf16),
            pltpu.VMEM((rounds, rows, feature), bf16),
            pltpu.VMEM((rows, feature), bf16),
            pltpu.VMEM((rounds, rows, feature), bf16),
            pltpu.VMEM((rounds, rows, feature), bf16),
            pltpu.VMEM((rows, rows), f32),
            pltpu.VMEM((kinds, feature, feature), bf16),
            pltpu.VMEM((kinds * feature, feature), f32),
            pltpu.VMEM((flat, lanes), bf16),
            pltpu.VMEM((chunks, na, rows_a, lanes), bf16),
            pltpu.VMEM((chunks, rows_a, lanes), bf16),
            pltpu.VMEM((chunks, nb, rows_b, lanes), bf16),
            pltpu.VMEM((flat, lanes), bf16),
            dma((5,)), dma((2 + chunks,)),
            dma((1,)), dma((rounds, parts)), dma((1,)), dma((rounds, parts)),
            dma((1,)), dma((chunks,)), dma((1,)), dma((chunks,)),
            dma((1,)), dma((chunks,)), dma((1,)), dma((chunks,)),
        ],
        compiler_params=pltpu.CompilerParams(
            collective_id=0, has_side_effects=True, vmem_limit_bytes=64 * 1024 * 1024
        ),
    )(rel_ids, entity, relations, edge_src, edge_dst)
    table = base - learn_rate * ret.astype(f32)
    sides = feature // lanes
    rel = rel.reshape(kinds, sides, feature, lanes).transpose(0, 2, 1, 3)
    return table, rel.reshape(kinds, feature, feature).astype(f32)


def solution(mesh):
    return jax.shard_map(
        functools.partial(shards, mesh.shape["gx"], mesh.shape["gy"]),
        mesh=mesh,
        in_specs=(
            P(("gx", "gy"), None),
            P(),
            P(None, ("gx", "gy")),
            P(None, ("gx", "gy")),
            P(None, ("gx", "gy")),
        ),
        out_specs=(P(("gx", "gy"), None), P()),
        check_vma=False,
    )
```

```python
import functools
import math

import jax
import jax.numpy as jnp
from jax import lax
from jax.experimental import pallas as pl
from jax.experimental.pallas import tpu as pltpu
from jax.sharding import PartitionSpec as P

learn_rate = 0.5
MESH = pl.DeviceIdType.MESH
f32, bf16 = jnp.float32, jnp.bfloat16
buckets = (("gy", 1), ("gx", 1), ("gy", -1))
lanes = 128
least_rows = 16


def matmul(left, right, left_dim, right_dim):
    return lax.dot_general(
        left, right, (((left_dim,), (right_dim,)), ((), ())), preferred_element_type=f32
    )


def chunk_of(count):
    for chunk in (1024, 512, 256, 128):
        if count % chunk == 0:
            return chunk
    return count


def kernel(
    na, nb, divisor, ids_in, x_in, rel_in, src_in, dst_in, table_out, rel_out,
    ids, rel, src, dst,
    x, xb, fetched, mapped, grads, returned, counts, relb, rel_acc, pieces,
    part_c, sum_c, part_x, part_sum, part_y, gathered,
    load_sem, store_sem,
    fetch_send, fetch_recv, ret_send, ret_recv, rsc_send, rsc_recv, rsx_send, rsx_recv,
    rsy_send, rsy_recv, agy_send, agy_recv, agx_send, agx_recv, agc_send, agc_recv,
):
    a, b = lax.axis_index("gx"), lax.axis_index("gy")
    rounds, groups = ids.shape
    rows, feature = x.shape
    kinds = rel.shape[0]
    block = rows // groups
    edges = src.shape[1]
    scaling = 1.0 / math.sqrt(rows)
    parts = fetch_recv.shape[1]
    rows_p = rows // parts
    chunks = part_x.shape[0]
    flat = gathered.shape[0]
    flat_k = flat // chunks
    rows_a = flat_k // na
    owners = min(nb, rows_a // least_rows)
    rows_b = rows_a // owners

    loads = [
        pltpu.make_async_copy(source, target, load_sem.at[i])
        for i, (source, target) in enumerate(
            ((x_in, x), (src_in, src), (dst_in, dst), (ids_in, ids), (rel_in, rel))
        )
    ]
    for load in loads:
        load.start()

    def owning(position):
        if owners == nb:
            return lambda body: body()
        return pl.when(position < owners)

    side_a = lax.rem(a, 2)
    pair = lax.div(a, 2)
    pairs = na // 2
    sibling = (a + 1 - 2 * side_a, b)

    def same_side(step):
        return 2 * lax.rem(pair + step + pairs, pairs) + side_a

    def other_side(step):
        return 2 * lax.rem(pair + step + pairs, pairs) + 1 - side_a

    def at_x(step):
        return lax.rem(a + step + na, na)

    def at_y(step):
        return lax.rem(b + step + nb, nb)

    barrier = pltpu.get_barrier_semaphore()
    for i in range(1, na):
        pl.semaphore_signal(barrier, inc=1, device_id=(at_x(i), b), device_id_type=MESH)
    for i in range(1, nb):
        pl.semaphore_signal(barrier, inc=1, device_id=(a, at_y(i)), device_id_type=MESH)

    def ring(turn, back):
        axis, offset = buckets[turn % len(buckets)]
        step = -offset if back else offset
        return (at_x(step), b) if axis == "gx" else (a, at_y(step))

    def part_of(c):
        return slice(c * rows_p, (c + 1) * rows_p)

    def fetch(turn, c):
        here = pl.ds(c * rows_p, rows_p)
        return pltpu.make_async_remote_copy(
            src_ref=xb.at[turn, here, :], dst_ref=fetched.at[turn, here, :],
            send_sem=fetch_send.at[0], recv_sem=fetch_recv.at[turn, c],
            device_id=ring(turn, False), device_id_type=MESH,
        )

    def give_back(turn, c):
        here = pl.ds(c * rows_p, rows_p)
        return pltpu.make_async_remote_copy(
            src_ref=grads.at[turn, here, :], dst_ref=returned.at[turn, here, :],
            send_sem=ret_send.at[0], recv_sem=ret_recv.at[turn, c],
            device_id=ring(turn, True), device_id_type=MESH,
        )

    def await_rows(count, sem):
        held = gathered.at[pl.ds(0, count), :]
        pltpu.make_async_copy(held, held, sem).wait()

    def await_owners(weight, sem):
        if owners == nb:
            await_rows((nb - 1) * weight, sem)
            return

        @pl.when(b >= owners)
        def _():
            await_rows(owners * weight, sem)

        if owners > 1:
            @pl.when(b < owners)
            def _():
                await_rows((owners - 1) * weight, sem)

    def count(turn, section, sections):
        chunk = chunk_of(edges)
        spots = lax.broadcasted_iota(jnp.int32, (rows, chunk), 0).astype(f32).astype(bf16)
        one, zero = jnp.ones((), bf16), jnp.zeros((), bf16)
        total = None
        starts = range(0, edges, chunk)
        size = -(-len(starts) // sections)
        for start in starts[section * size : (section + 1) * size]:
            s = src[turn : turn + 1, start : start + chunk].astype(f32).astype(bf16)
            t = dst[turn : turn + 1, start : start + chunk].astype(f32).astype(bf16)
            s_hot = jnp.where(spots == s, one, zero)
            t_hot = jnp.where(spots == t, one, zero)
            term = matmul(s_hot, t_hot, 1, 1)
            total = term if total is None else total + term
        if total is not None:
            counts[...] = counts[...] + total if section > 0 else total

    def block_at(k, x_pos):
        return pl.ds(pl.multiple_of(k * flat_k + x_pos * rows_a, rows_a), rows_a)

    def scatter_c(k, i):
        return pltpu.make_async_remote_copy(
            src_ref=pieces.at[block_at(k, other_side(i)), :], dst_ref=part_c.at[k, i],
            send_sem=rsc_send.at[0], recv_sem=rsc_recv.at[k],
            device_id=sibling, device_id_type=MESH,
        )

    def scatter_x(k, i):
        return pltpu.make_async_remote_copy(
            src_ref=sum_c.at[k, i], dst_ref=part_x.at[k, i],
            send_sem=rsx_send.at[0], recv_sem=rsx_recv.at[k],
            device_id=(same_side(i), b), device_id_type=MESH,
        )

    def scatter_y(k, i):
        return pltpu.make_async_remote_copy(
            src_ref=part_sum.at[k, pl.ds(pl.multiple_of(at_y(i) * rows_b, rows_b), rows_b), :],
            dst_ref=part_y.at[k, i],
            send_sem=rsy_send.at[0], recv_sem=rsy_recv.at[k],
            device_id=(a, at_y(i)), device_id_type=MESH,
        )

    def spot(k, y_pos):
        start = k * flat_k + a * rows_a + y_pos * rows_b
        return pl.ds(pl.multiple_of(start, rows_b), rows_b)

    def gather_y(k, i, y_pos):
        return pltpu.make_async_remote_copy(
            src_ref=gathered.at[spot(k, y_pos), :], dst_ref=gathered.at[spot(k, y_pos), :],
            send_sem=agy_send.at[0], recv_sem=agy_recv.at[k],
            device_id=(a, at_y(i)), device_id_type=MESH,
        )

    def gather_x(k, i):
        here = block_at(k, a)
        return pltpu.make_async_remote_copy(
            src_ref=gathered.at[here, :], dst_ref=gathered.at[here, :],
            send_sem=agx_send.at[0], recv_sem=agx_recv.at[k],
            device_id=(same_side(i), b), device_id_type=MESH,
        )

    def gather_c(k, x_pos):
        here = block_at(k, x_pos)
        return pltpu.make_async_remote_copy(
            src_ref=gathered.at[here, :], dst_ref=gathered.at[here, :],
            send_sem=agc_send.at[0], recv_sem=agc_recv.at[k],
            device_id=sibling, device_id_type=MESH,
        )

    loads[0].wait()
    xb[0] = x[...].astype(bf16)
    pl.semaphore_wait(barrier, na + nb - 2)
    for c in range(parts):
        fetch(0, c).start()
    for load in loads[1:]:
        load.wait()
    for kind in range(kinds):
        relb[kind] = rel[kind].astype(bf16)

    def map_rows(turn):
        for g in range(groups):
            span = slice(g * block, (g + 1) * block)
            mapped[span, :] = matmul(xb[turn, span, :], relb[ids[turn, g]], 1, 0).astype(bf16)

    map_rows(0)
    count(0, 0, 1)

    for turn in range(rounds):
        last = turn == rounds - 1
        if turn > 0:
            map_rows(turn)
            relation_term()
            count(turn, 1, 2)
        turned = xb[turn].T
        column = lax.broadcasted_iota(jnp.int32, (1, rows), 1) // block
        kind_of = jnp.zeros((1, rows), jnp.int32)
        for g in range(groups):
            kind_of = jnp.where(column == g, ids[turn, g], kind_of)
        here_b = mapped[...]

        slopes = []
        total = None
        for c in range(parts):
            fetch(turn, c).wait_recv()
            their = fetched[turn, part_of(c), :]
            scores = matmul(here_b, their, 1, 1)
            slope = (
                (0.5 * jnp.tanh(0.5 * scores) + 0.5 - counts[:, part_of(c)]) * scaling
            ).astype(bf16)
            slopes.append(slope)
            if not last:
                grads[turn, part_of(c), :] = matmul(slope, here_b, 0, 0).astype(bf16)
                give_back(turn, c).start()
            term = matmul(slope, their, 1, 0)
            total = term if total is None else total + term
        pulled = total.astype(bf16)

        def relation_term(turn=turn, last=last, turned=turned, kind_of=kind_of, pulled=pulled):
            for kind in range(kinds):
                chosen = turned * (kind_of == kind).astype(f32).astype(bf16)
                term = matmul(chosen, pulled, 1, 0)
                place = slice(kind * feature, (kind + 1) * feature)
                if turn > 0:
                    term = term + rel_acc[place, :]
                if not last:
                    rel_acc[place, :] = term
                    continue
                term = (term * (1.0 / divisor)).astype(bf16)
                for side in range(feature // lanes):
                    start = kind * (flat // kinds) + side * feature
                    pieces[start : start + feature, :] = term[:, side * lanes : (side + 1) * lanes]
                if (kind + 1) % (kinds // chunks) == 0:
                    for i in range(pairs):
                        scatter_c(kind // (kinds // chunks), i).start()

        if last:
            relation_term()
            for c in range(parts):
                grads[turn, part_of(c), :] = matmul(slopes[c], here_b, 0, 0).astype(bf16)
                give_back(turn, c).start()
        for g in range(groups):
            span = slice(g * block, (g + 1) * block)
            x[span, :] = x[span, :] - learn_rate * matmul(pulled[span, :], relb[ids[turn, g]], 1, 1)
        if not last:
            count(turn + 1, 0, 2)
            for c in range(parts):
                give_back(turn, c).wait_recv()
                moved = x[part_of(c), :] - learn_rate * returned[turn, part_of(c), :].astype(f32)
                x[part_of(c), :] = moved
                xb[turn + 1, part_of(c), :] = moved.astype(bf16)
                fetch(turn + 1, c).start()

    def pair_sum(k, i):
        return pieces[block_at(k, same_side(i)), :].astype(f32) + part_c[k, i].astype(f32)

    def reduce_c(k):
        await_rows(pairs * rows_a, rsc_recv.at[k])
        for i in range(1, pairs):
            sum_c[k, i] = pair_sum(k, i).astype(bf16)
            scatter_x(k, i).start()

    def reduce_x(k):
        own = pair_sum(k, 0)
        if pairs > 1:
            await_rows((pairs - 1) * rows_a, rsx_recv.at[k])
        for i in range(1, pairs):
            own = own + part_x[k, i].astype(f32)
        part_sum[k] = own.astype(bf16)
        for i in range(1, nb):
            @owning(at_y(i))
            def _():
                scatter_y(k, i).start()

    def reduce_y(k):
        @owning(b)
        def _():
            mine = part_sum[k, pl.ds(pl.multiple_of(b * rows_b, rows_b), rows_b), :].astype(f32)
            await_rows((nb - 1) * rows_b, rsy_recv.at[k])
            for i in range(1, nb):
                mine = mine + part_y[k, i].astype(f32)
            gathered[spot(k, b), :] = mine.astype(bf16)
            for i in range(1, nb):
                gather_y(k, i, b).start()

    def spread(k):
        await_owners(rows_b, agy_recv.at[k])
        for i in range(1, pairs):
            gather_x(k, i).start()
        gather_c(k, a).start()

    def forward(k):
        if pairs > 1:
            await_rows((pairs - 1) * rows_a, agx_recv.at[k])
        for i in range(1, pairs):
            gather_c(k, same_side(-i)).start()

    stages = (reduce_c, reduce_x, reduce_y, spread, forward)
    for step in range(chunks + len(stages) - 1):
        if step == chunks + len(stages) - 2:
            for c in range(parts):
                give_back(rounds - 1, c).wait_recv()
            x[...] = x[...] - learn_rate * returned[rounds - 1].astype(f32)
            store_table = pltpu.make_async_copy(x, table_out, store_sem.at[0])
            store_table.start()
        for number, stage in enumerate(stages):
            if 0 <= step - number < chunks:
                stage(step - number)

    stores = [store_table]
    for k in range(chunks):
        await_rows(pairs * rows_a, agc_recv.at[k])
        here = pl.ds(k * flat_k, flat_k)
        store = pltpu.make_async_copy(gathered.at[here, :], rel_out.at[here, :], store_sem.at[1 + k])
        store.start()
        stores.append(store)

    pltpu.make_async_copy(fetched, fetched, fetch_send.at[0]).wait()
    pltpu.make_async_copy(fetched, fetched, ret_send.at[0]).wait()
    await_rows(chunks * pairs * rows_a, rsc_send.at[0])
    await_rows(chunks * pairs * rows_a, agc_send.at[0])
    if pairs > 1:
        await_rows(chunks * (pairs - 1) * rows_a, rsx_send.at[0])
        await_rows(chunks * (pairs - 1) * rows_a, agx_send.at[0])
    await_owners(chunks * rows_b, rsy_send.at[0])

    @owning(b)
    def _():
        await_rows(chunks * (nb - 1) * rows_b, agy_send.at[0])

    for store in stores:
        store.wait()


def shards(na, nb, entity, relations, rel_ids, edge_src, edge_dst):
    rows, feature = entity.shape
    rounds, groups = rel_ids.shape
    kinds = relations.shape[0]
    parts = 2
    chunks = 2 if kinds % 2 == 0 else 1
    flat = kinds * feature * feature // lanes
    rows_a = flat // chunks // na
    rows_b = rows_a // min(nb, rows_a // least_rows)
    divisor = math.sqrt(rounds * na * nb)
    dma = pltpu.SemaphoreType.DMA
    in_hbm = pl.BlockSpec(memory_space=pltpu.HBM)
    table, rel = pl.pallas_call(
        functools.partial(kernel, na, nb, divisor),
        out_shape=(
            jax.ShapeDtypeStruct((rows, feature), f32),
            jax.ShapeDtypeStruct((flat, lanes), bf16),
        ),
        in_specs=[in_hbm] * 5,
        out_specs=(in_hbm,) * 2,
        scratch_shapes=[
            pltpu.SMEM(rel_ids.shape, jnp.int32),
            pltpu.VMEM(relations.shape, f32),
            pltpu.VMEM(edge_src.shape, jnp.int32),
            pltpu.VMEM(edge_dst.shape, jnp.int32),
            pltpu.VMEM((rows, feature), f32),
            pltpu.VMEM((rounds, rows, feature), bf16),
            pltpu.VMEM((rounds, rows, feature), bf16),
            pltpu.VMEM((rows, feature), bf16),
            pltpu.VMEM((rounds, rows, feature), bf16),
            pltpu.VMEM((rounds, rows, feature), bf16),
            pltpu.VMEM((rows, rows), f32),
            pltpu.VMEM((kinds, feature, feature), bf16),
            pltpu.VMEM((kinds * feature, feature), f32),
            pltpu.VMEM((flat, lanes), bf16),
            pltpu.VMEM((chunks, na // 2, rows_a, lanes), bf16),
            pltpu.VMEM((chunks, na // 2, rows_a, lanes), bf16),
            pltpu.VMEM((chunks, na // 2, rows_a, lanes), bf16),
            pltpu.VMEM((chunks, rows_a, lanes), bf16),
            pltpu.VMEM((chunks, nb, rows_b, lanes), bf16),
            pltpu.VMEM((flat, lanes), bf16),
            dma((5,)), dma((1 + chunks,)),
            dma((1,)), dma((rounds, parts)), dma((1,)), dma((rounds, parts)),
            dma((1,)), dma((chunks,)), dma((1,)), dma((chunks,)),
            dma((1,)), dma((chunks,)), dma((1,)), dma((chunks,)),
            dma((1,)), dma((chunks,)), dma((1,)), dma((chunks,)),
        ],
        compiler_params=pltpu.CompilerParams(
            collective_id=0, has_side_effects=True, vmem_limit_bytes=64 * 1024 * 1024
        ),
    )(rel_ids, entity, relations, edge_src, edge_dst)
    sides = feature // lanes
    rel = rel.reshape(kinds, sides, feature, lanes).transpose(0, 2, 1, 3)
    return table, rel.reshape(kinds, feature, feature).astype(f32)


def solution(mesh):
    return jax.shard_map(
        functools.partial(shards, mesh.shape["gx"], mesh.shape["gy"]),
        mesh=mesh,
        in_specs=(
            P(("gx", "gy"), None),
            P(),
            P(None, ("gx", "gy")),
            P(None, ("gx", "gy")),
            P(None, ("gx", "gy")),
        ),
        out_specs=(P(("gx", "gy"), None), P()),
        check_vma=False,
    )
```

```python
import functools
import math

import jax
import jax.numpy as jnp
from jax import lax
from jax.experimental import pallas as pl
from jax.experimental.pallas import tpu as pltpu
from jax.sharding import PartitionSpec as P

learn_rate = 0.5
MESH = pl.DeviceIdType.MESH
f32, bf16 = jnp.float32, jnp.bfloat16
buckets = (("gy", 1), ("gx", 1), ("gy", -1))
lanes = 128
least_rows = 16


def matmul(left, right, left_dim, right_dim):
    return lax.dot_general(
        left, right, (((left_dim,), (right_dim,)), ((), ())), preferred_element_type=f32
    )


def chunk_of(count):
    for chunk in (1024, 512, 256, 128):
        if count % chunk == 0:
            return chunk
    return count


def kernel(
    na, nb, divisor, ids_in, x_in, rel_in, src_in, dst_in, table_out, rel_out,
    ids, rel, src, dst,
    x, xb, fetched, mapped, grads, returned, counts, relb, rel_acc, pieces,
    part_c, sum_c, part_x, part_sum, part_y, gathered,
    load_sem, store_sem,
    fetch_send, fetch_recv, ret_send, ret_recv, rsc_send, rsc_recv, rsx_send, rsx_recv,
    rsy_send, rsy_recv, agy_send, agy_recv, agx_send, agx_recv, agc_send, agc_recv,
):
    a, b = lax.axis_index("gx"), lax.axis_index("gy")
    rounds, groups = ids.shape
    rows, feature = x.shape
    kinds = rel.shape[0]
    block = rows // groups
    edges = src.shape[1]
    scaling = 1.0 / math.sqrt(rows)
    parts = fetch_recv.shape[1]
    rows_p = rows // parts
    chunks = part_x.shape[0]
    flat = gathered.shape[0]
    flat_k = flat // chunks
    rows_a = flat_k // na
    owners = min(nb, rows_a // least_rows)
    rows_b = rows_a // owners

    loads = [
        pltpu.make_async_copy(source, target, load_sem.at[i])
        for i, (source, target) in enumerate(
            ((x_in, x), (src_in, src), (dst_in, dst), (ids_in, ids), (rel_in, rel))
        )
    ]
    for load in loads:
        load.start()

    def owning(position):
        if owners == nb:
            return lambda body: body()
        return pl.when(position < owners)

    side_a = lax.rem(a, 2)
    pair = lax.div(a, 2)
    pairs = na // 2
    sibling = (a + 1 - 2 * side_a, b)

    def same_side(step):
        return 2 * lax.rem(pair + step + pairs, pairs) + side_a

    def other_side(step):
        return 2 * lax.rem(pair + step + pairs, pairs) + 1 - side_a

    def at_x(step):
        return lax.rem(a + step + na, na)

    def at_y(step):
        return lax.rem(b + step + nb, nb)

    barrier = pltpu.get_barrier_semaphore()
    for i in range(1, na):
        pl.semaphore_signal(barrier, inc=1, device_id=(at_x(i), b), device_id_type=MESH)
    for i in range(1, nb):
        pl.semaphore_signal(barrier, inc=1, device_id=(a, at_y(i)), device_id_type=MESH)

    def ring(turn, back):
        axis, offset = buckets[turn % len(buckets)]
        step = -offset if back else offset
        return (at_x(step), b) if axis == "gx" else (a, at_y(step))

    def part_of(c):
        return slice(c * rows_p, (c + 1) * rows_p)

    def fetch(turn, c):
        here = pl.ds(c * rows_p, rows_p)
        return pltpu.make_async_remote_copy(
            src_ref=xb.at[turn, here, :], dst_ref=fetched.at[turn, here, :],
            send_sem=fetch_send.at[0], recv_sem=fetch_recv.at[turn, c],
            device_id=ring(turn, False), device_id_type=MESH,
        )

    def give_back(turn, c):
        here = pl.ds(c * rows_p, rows_p)
        return pltpu.make_async_remote_copy(
            src_ref=grads.at[turn, here, :], dst_ref=returned.at[turn, here, :],
            send_sem=ret_send.at[0], recv_sem=ret_recv.at[turn, c],
            device_id=ring(turn, True), device_id_type=MESH,
        )

    def await_rows(count, sem):
        held = gathered.at[pl.ds(0, count), :]
        pltpu.make_async_copy(held, held, sem).wait()

    def await_owners(weight, sem):
        if owners == nb:
            await_rows((nb - 1) * weight, sem)
            return

        @pl.when(b >= owners)
        def _():
            await_rows(owners * weight, sem)

        if owners > 1:
            @pl.when(b < owners)
            def _():
                await_rows((owners - 1) * weight, sem)

    def count(turn, first, thirds):
        chunk = chunk_of(edges)
        spots = lax.broadcasted_iota(jnp.int32, (rows, chunk), 0).astype(f32).astype(bf16)
        one, zero = jnp.ones((), bf16), jnp.zeros((), bf16)
        total = None
        starts = range(0, edges, chunk)
        cut = len(starts) * thirds // 3
        for start in starts[:cut] if first else starts[cut:]:
            s = src[turn : turn + 1, start : start + chunk].astype(f32).astype(bf16)
            t = dst[turn : turn + 1, start : start + chunk].astype(f32).astype(bf16)
            s_hot = jnp.where(spots == s, one, zero)
            t_hot = jnp.where(spots == t, one, zero)
            term = matmul(s_hot, t_hot, 1, 1)
            total = term if total is None else total + term
        if total is None:
            total = jnp.zeros(counts.shape, f32)
        counts[...] = total if first else counts[...] + total

    def block_at(k, x_pos):
        return pl.ds(pl.multiple_of(k * flat_k + x_pos * rows_a, rows_a), rows_a)

    def scatter_c(k, i):
        return pltpu.make_async_remote_copy(
            src_ref=pieces.at[block_at(k, other_side(i)), :], dst_ref=part_c.at[k, i],
            send_sem=rsc_send.at[0], recv_sem=rsc_recv.at[k],
            device_id=sibling, device_id_type=MESH,
        )

    def scatter_x(k, i):
        return pltpu.make_async_remote_copy(
            src_ref=sum_c.at[k, i], dst_ref=part_x.at[k, i],
            send_sem=rsx_send.at[0], recv_sem=rsx_recv.at[k],
            device_id=(same_side(i), b), device_id_type=MESH,
        )

    def scatter_y(k, i):
        return pltpu.make_async_remote_copy(
            src_ref=part_sum.at[k, pl.ds(pl.multiple_of(at_y(i) * rows_b, rows_b), rows_b), :],
            dst_ref=part_y.at[k, i],
            send_sem=rsy_send.at[0], recv_sem=rsy_recv.at[k],
            device_id=(a, at_y(i)), device_id_type=MESH,
        )

    def spot(k, y_pos):
        start = k * flat_k + a * rows_a + y_pos * rows_b
        return pl.ds(pl.multiple_of(start, rows_b), rows_b)

    def gather_y(k, i, y_pos):
        return pltpu.make_async_remote_copy(
            src_ref=gathered.at[spot(k, y_pos), :], dst_ref=gathered.at[spot(k, y_pos), :],
            send_sem=agy_send.at[0], recv_sem=agy_recv.at[k],
            device_id=(a, at_y(i)), device_id_type=MESH,
        )

    def gather_x(k, i):
        here = block_at(k, a)
        return pltpu.make_async_remote_copy(
            src_ref=gathered.at[here, :], dst_ref=gathered.at[here, :],
            send_sem=agx_send.at[0], recv_sem=agx_recv.at[k],
            device_id=(same_side(i), b), device_id_type=MESH,
        )

    def gather_c(k, x_pos):
        here = block_at(k, x_pos)
        return pltpu.make_async_remote_copy(
            src_ref=gathered.at[here, :], dst_ref=gathered.at[here, :],
            send_sem=agc_send.at[0], recv_sem=agc_recv.at[k],
            device_id=sibling, device_id_type=MESH,
        )

    loads[0].wait()
    xb[0] = x[...].astype(bf16)
    pl.semaphore_wait(barrier, na + nb - 2)
    for c in range(parts):
        fetch(0, c).start()
    for load in loads[1:]:
        load.wait()
    for kind in range(kinds):
        relb[kind] = rel[kind].astype(bf16)

    def map_rows(turn):
        for g in range(groups):
            span = slice(g * block, (g + 1) * block)
            mapped[span, :] = matmul(xb[turn, span, :], relb[ids[turn, g]], 1, 0).astype(bf16)

    map_rows(0)
    count(0, True, 3)

    for turn in range(rounds):
        last = turn == rounds - 1
        if turn > 0:
            map_rows(turn)
            if not long_way:
                relation_term()
            count(turn, False, 2 if long_way else 1)
        turned = xb[turn].T
        column = lax.broadcasted_iota(jnp.int32, (1, rows), 1) // block
        kind_of = jnp.zeros((1, rows), jnp.int32)
        for g in range(groups):
            kind_of = jnp.where(column == g, ids[turn, g], kind_of)
        here_b = mapped[...]

        slopes = []
        total = None
        for c in range(parts):
            fetch(turn, c).wait_recv()
            their = fetched[turn, part_of(c), :]
            scores = matmul(here_b, their, 1, 1)
            slope = (
                (0.5 * jnp.tanh(0.5 * scores) + 0.5 - counts[:, part_of(c)]) * scaling
            ).astype(bf16)
            slopes.append(slope)
            if not last:
                grads[turn, part_of(c), :] = matmul(slope, here_b, 0, 0).astype(bf16)
                give_back(turn, c).start()
            term = matmul(slope, their, 1, 0)
            total = term if total is None else total + term
        pulled = total.astype(bf16)

        def relation_term(turn=turn, last=last, turned=turned, kind_of=kind_of, pulled=pulled):
            for kind in range(kinds):
                chosen = turned * (kind_of == kind).astype(f32).astype(bf16)
                term = matmul(chosen, pulled, 1, 0)
                place = slice(kind * feature, (kind + 1) * feature)
                if turn > 0:
                    term = term + rel_acc[place, :]
                if not last:
                    rel_acc[place, :] = term
                    continue
                term = (term * (1.0 / divisor)).astype(bf16)
                for side in range(feature // lanes):
                    start = kind * (flat // kinds) + side * feature
                    pieces[start : start + feature, :] = term[:, side * lanes : (side + 1) * lanes]
                if (kind + 1) % (kinds // chunks) == 0:
                    for i in range(pairs):
                        scatter_c(kind // (kinds // chunks), i).start()

        if last:
            relation_term()
            for c in range(parts):
                grads[turn, part_of(c), :] = matmul(slopes[c], here_b, 0, 0).astype(bf16)
                give_back(turn, c).start()
        for g in range(groups):
            span = slice(g * block, (g + 1) * block)
            x[span, :] = x[span, :] - learn_rate * matmul(pulled[span, :], relb[ids[turn, g]], 1, 1)
        if not last:
            long_way = buckets[turn % len(buckets)][0] == "gy"
            if long_way:
                relation_term()
            count(turn + 1, True, 2 if long_way else 1)
            for c in range(parts):
                give_back(turn, c).wait_recv()
                moved = x[part_of(c), :] - learn_rate * returned[turn, part_of(c), :].astype(f32)
                x[part_of(c), :] = moved
                xb[turn + 1, part_of(c), :] = moved.astype(bf16)
                fetch(turn + 1, c).start()

    def pair_sum(k, i):
        return pieces[block_at(k, same_side(i)), :].astype(f32) + part_c[k, i].astype(f32)

    def reduce_c(k):
        await_rows(pairs * rows_a, rsc_recv.at[k])
        for i in range(1, pairs):
            sum_c[k, i] = pair_sum(k, i).astype(bf16)
            scatter_x(k, i).start()

    def reduce_x(k):
        own = pair_sum(k, 0)
        if pairs > 1:
            await_rows((pairs - 1) * rows_a, rsx_recv.at[k])
        for i in range(1, pairs):
            own = own + part_x[k, i].astype(f32)
        part_sum[k] = own.astype(bf16)
        for i in range(1, nb):
            @owning(at_y(i))
            def _():
                scatter_y(k, i).start()

    def reduce_y(k):
        @owning(b)
        def _():
            mine = part_sum[k, pl.ds(pl.multiple_of(b * rows_b, rows_b), rows_b), :].astype(f32)
            await_rows((nb - 1) * rows_b, rsy_recv.at[k])
            for i in range(1, nb):
                mine = mine + part_y[k, i].astype(f32)
            gathered[spot(k, b), :] = mine.astype(bf16)
            for i in range(1, nb):
                gather_y(k, i, b).start()

    def spread(k):
        await_owners(rows_b, agy_recv.at[k])
        for i in range(1, pairs):
            gather_x(k, i).start()
        gather_c(k, a).start()

    def forward(k):
        if pairs > 1:
            await_rows((pairs - 1) * rows_a, agx_recv.at[k])
        for i in range(1, pairs):
            gather_c(k, same_side(-i)).start()

    stages = (reduce_c, reduce_x, reduce_y, spread, forward)
    for step in range(chunks + len(stages) - 1):
        if step == chunks + len(stages) - 2:
            for c in range(parts):
                give_back(rounds - 1, c).wait_recv()
            x[...] = x[...] - learn_rate * returned[rounds - 1].astype(f32)
            store_table = pltpu.make_async_copy(x, table_out, store_sem.at[0])
            store_table.start()
        for number, stage in enumerate(stages):
            if 0 <= step - number < chunks:
                stage(step - number)

    stores = [store_table]
    for k in range(chunks):
        await_rows(pairs * rows_a, agc_recv.at[k])
        here = pl.ds(k * flat_k, flat_k)
        store = pltpu.make_async_copy(gathered.at[here, :], rel_out.at[here, :], store_sem.at[1 + k])
        store.start()
        stores.append(store)

    pltpu.make_async_copy(fetched, fetched, fetch_send.at[0]).wait()
    pltpu.make_async_copy(fetched, fetched, ret_send.at[0]).wait()
    await_rows(chunks * pairs * rows_a, rsc_send.at[0])
    await_rows(chunks * pairs * rows_a, agc_send.at[0])
    if pairs > 1:
        await_rows(chunks * (pairs - 1) * rows_a, rsx_send.at[0])
        await_rows(chunks * (pairs - 1) * rows_a, agx_send.at[0])
    await_owners(chunks * rows_b, rsy_send.at[0])

    @owning(b)
    def _():
        await_rows(chunks * (nb - 1) * rows_b, agy_send.at[0])

    for store in stores:
        store.wait()


def shards(na, nb, entity, relations, rel_ids, edge_src, edge_dst):
    rows, feature = entity.shape
    rounds, groups = rel_ids.shape
    kinds = relations.shape[0]
    parts = 2
    chunks = 2 if kinds % 2 == 0 else 1
    flat = kinds * feature * feature // lanes
    rows_a = flat // chunks // na
    rows_b = rows_a // min(nb, rows_a // least_rows)
    divisor = math.sqrt(rounds * na * nb)
    dma = pltpu.SemaphoreType.DMA
    in_hbm = pl.BlockSpec(memory_space=pltpu.HBM)
    table, rel = pl.pallas_call(
        functools.partial(kernel, na, nb, divisor),
        out_shape=(
            jax.ShapeDtypeStruct((rows, feature), f32),
            jax.ShapeDtypeStruct((flat, lanes), bf16),
        ),
        in_specs=[in_hbm] * 5,
        out_specs=(in_hbm,) * 2,
        scratch_shapes=[
            pltpu.SMEM(rel_ids.shape, jnp.int32),
            pltpu.VMEM(relations.shape, f32),
            pltpu.VMEM(edge_src.shape, jnp.int32),
            pltpu.VMEM(edge_dst.shape, jnp.int32),
            pltpu.VMEM((rows, feature), f32),
            pltpu.VMEM((rounds, rows, feature), bf16),
            pltpu.VMEM((rounds, rows, feature), bf16),
            pltpu.VMEM((rows, feature), bf16),
            pltpu.VMEM((rounds, rows, feature), bf16),
            pltpu.VMEM((rounds, rows, feature), bf16),
            pltpu.VMEM((rows, rows), f32),
            pltpu.VMEM((kinds, feature, feature), bf16),
            pltpu.VMEM((kinds * feature, feature), f32),
            pltpu.VMEM((flat, lanes), bf16),
            pltpu.VMEM((chunks, na // 2, rows_a, lanes), bf16),
            pltpu.VMEM((chunks, na // 2, rows_a, lanes), bf16),
            pltpu.VMEM((chunks, na // 2, rows_a, lanes), bf16),
            pltpu.VMEM((chunks, rows_a, lanes), bf16),
            pltpu.VMEM((chunks, nb, rows_b, lanes), bf16),
            pltpu.VMEM((flat, lanes), bf16),
            dma((5,)), dma((1 + chunks,)),
            dma((1,)), dma((rounds, parts)), dma((1,)), dma((rounds, parts)),
            dma((1,)), dma((chunks,)), dma((1,)), dma((chunks,)),
            dma((1,)), dma((chunks,)), dma((1,)), dma((chunks,)),
            dma((1,)), dma((chunks,)), dma((1,)), dma((chunks,)),
        ],
        compiler_params=pltpu.CompilerParams(
            collective_id=0, has_side_effects=True, vmem_limit_bytes=64 * 1024 * 1024
        ),
    )(rel_ids, entity, relations, edge_src, edge_dst)
    sides = feature // lanes
    rel = rel.reshape(kinds, sides, feature, lanes).transpose(0, 2, 1, 3)
    return table, rel.reshape(kinds, feature, feature).astype(f32)


def solution(mesh):
    return jax.shard_map(
        functools.partial(shards, mesh.shape["gx"], mesh.shape["gy"]),
        mesh=mesh,
        in_specs=(
            P(("gx", "gy"), None),
            P(),
            P(None, ("gx", "gy")),
            P(None, ("gx", "gy")),
            P(None, ("gx", "gy")),
        ),
        out_specs=(P(("gx", "gy"), None), P()),
        check_vma=False,
    )
```
